256 devices in a mesh: tok: 32 (over x_lo, z, core), feat: 8 (over x_hi, y).
Axes of the slice: x: 4 (x_hi: 2, x_lo: 2; x = x_hi * 2 + x_lo), y: 4, z: 8, core: 2. Of those that a mesh axis runs over, the one named last changes fastest.
Arguments:
- teacher: bfloat16 [8192, 8192], P('tok', 'feat')
- student: bfloat16 [8192, 5120], P('tok', 'feat')
Outputs:
- loss: float32 [], replicated
- grad_student: float32 [8192, 5120], P('tok', 'feat')
All inputs are finite; a program needn't handle non-finite values.
Results may differ from the reference program's by a relative error of at most 0.0031.
Values may be sent and summed in bfloat16 or wider, within the bound.
A program may use at most 128 MiB of HBM per device.

```python
import jax
import jax.numpy as jnp
from jax import lax

DT = 8192
DS = 5120
TOKENS = 8192


def row_scales(key):
    base = jax.random.uniform(jax.random.fold_in(key, 11), (TOKENS, 1), jnp.float32)
    ramp = jnp.sqrt(1.0 + 2.0 * jnp.arange(TOKENS, dtype=jnp.float32)[:, None] / TOKENS)
    return 10.0 ** base * ramp


def draw_features(key, width, salt, factor):
    rows = row_scales(key)
    cols = 10.0 ** jax.random.uniform(jax.random.fold_in(key, salt), (1, width), jnp.float32)
    noise_key = jax.random.fold_in(key, salt + 1)
    values = jax.random.normal(noise_key, (TOKENS, width), jnp.float32)
    return values * rows * cols * factor


def draw_teacher(key, part):
    return draw_features(key, DT, 21, 0.1).astype(jnp.bfloat16)


def draw_student(key, part):
    return draw_features(key, DS, 41, 0.1).astype(jnp.bfloat16)


def setup_inputs(seed: int = 0) -> dict:
    key_of = jax.random.split(jax.random.key(seed), 3)
    teacher = draw_teacher(jax.random.fold_in(key_of[2], 71), 0)
    student = draw_student(jax.random.fold_in(key_of[2], 71), 0)
    return {"teacher": teacher, "student": student}


def reference(teacher, student):
    kern = lax.dot_general(teacher, teacher, (((1,), (1,)), ((), ())), preferred_element_type=jnp.float32)
    lern = lax.dot_general(student, student, (((1,), (1,)), ((), ())), preferred_element_type=jnp.float32)
    cross = jnp.sum(kern * lern)
    knorm = jnp.sqrt(jnp.sum(kern * kern))
    lnorm = jnp.sqrt(jnp.sum(lern * lern))
    loss = -cross / (knorm * lnorm)
    weights = (-kern / (knorm * lnorm) + cross * lern / (knorm * lnorm ** 3)).astype(jnp.bfloat16)
    scale = 2.0 * TOKENS * DS
    grad_student = scale * lax.dot_general(weights, student, (((0,), (0,)), ((), ())), preferred_element_type=jnp.float32)
    return (loss, grad_student)
```

```python
import functools

import jax
import jax.numpy as jnp
from jax import lax
from jax.experimental import pallas as pl
from jax.experimental.pallas import tpu as pltpu
from jax.sharding import PartitionSpec as P

TOKENS = 8192
DS = 5120
MESH = pl.DeviceIdType.MESH
F32 = jnp.float32
BF16 = jnp.bfloat16


def slot(k):
    return k if k <= 4 else 12 - k


def kernel(
    t_ref, s_ref, loss_ref, grad_ref,
    tb, sb, stage, rs, own, total, wn, wt, tst, red, redr, acc,
    t_ring, t_core, t_ring_out, t_core_out,
    s_ring, s_core, s_ring_out, s_core_out, x_out,
    rs_in, rs_out, red_in, red_out, tr_in, tr_out, agn_in, agn_out, agt_in, agt_out,
):
    tok = lax.axis_index("tok")
    feat = lax.axis_index("feat")
    core = lax.rem(tok, 2)
    z = lax.rem(tok // 2, 8)
    xl = tok // 16
    y = lax.rem(feat, 4)
    xh = feat // 4

    def tok_of(x_lo, zz, c):
        return (x_lo * 8 + lax.rem(zz + 16, 8)) * 2 + c

    z_down = (tok_of(xl, z - 1, core), feat)
    z_up = (tok_of(xl, z + 1, core), feat)
    x_other = (tok_of(1 - xl, z, core), feat)
    sibling = (tok_of(xl, z, 1 - core), feat)

    def feat_peer(p):
        return lax.rem(feat + p, 8)

    swapped = core * 4 + y

    barrier = pltpu.get_barrier_semaphore()

    def greet(device):
        pl.semaphore_signal(barrier, inc=1, device_id=device, device_id_type=MESH)

    for p in range(1, 8):
        greet((tok, feat_peer(p)))
        greet((tok_of(xl, z + p, core), feat))
    for device in (x_other, sibling, (tok_of(1 - xl, z, 1 - core), feat)):
        greet(device)
    for s in (1, 2, 3):
        for sign in (s, -s):
            greet((tok_of(xl, z + sign, xh), swapped))
            greet((tok_of(1 - xl, z + sign, xh), swapped))
    pl.semaphore_wait(barrier, 29)

    def send(src, dst, out_sem, in_sem, device):
        pltpu.make_async_remote_copy(
            src_ref=src, dst_ref=dst, send_sem=out_sem, recv_sem=in_sem, device_id=device, device_id_type=MESH
        ).start()

    def wait(ref, sem):
        pltpu.make_async_copy(ref, ref, sem).wait()

    T = (t_ref, tb, t_ring, t_core, t_ring_out, t_core_out, 4)
    S = (s_ref, sb, s_ring, s_core, s_ring_out, s_core_out, 7)

    def launch(kind, index):
        src, buf, ring, cores, ring_out, core_out, last = kind
        for h in range(2):
            a = 2 * core + h
            rows = src.at[h * 128 : (h + 1) * 128]
            send(rows, buf.at[a, 0, 1], x_out.at[index], ring.at[0, 1, h], x_other)
            send(rows, buf.at[a, 1, 0], ring_out.at[0], ring.at[1, 0, h], z_down)
        for h in range(2):
            a = 2 * core + h
            rows = src.at[h * 128 : (h + 1) * 128]
            send(rows, buf.at[a, 0, 0], core_out.at[0], cores.at[0], sibling)
            buf[a, 0, 0] = src[h * 128 : (h + 1) * 128]

    def relay(kind, k):
        src, buf, ring, cores, ring_out, core_out, last = kind
        here, there = slot(k), slot(k + 1)
        for h in range(2):
            a = 2 * core + h
            for side in (0, 1) if k else (1,):
                block = buf.at[a, here, side]
                wait(block, ring.at[here, side, h])
                if k < last:
                    to = z_up if side else z_down
                    send(block, buf.at[a, there, side], ring_out.at[k], ring.at[there, side, h], to)
                send(block, block, core_out.at[here], cores.at[here], sibling)

    def have(kind, k):
        wait(kind[1].at[0:2, slot(k)], kind[3].at[slot(k)])

    def partials(kind, s, j):
        src, buf = kind[0], kind[1]

        @pl.loop(0, 4)
        def _(p):
            a = lax.rem(feat // 2 + p, 4)
            rows = buf[a, s].reshape(256, src.shape[1])
            x = lax.dot_general(src[...], rows, (((1,), (1,)), ((), ())), preferred_element_type=F32)
            for b in range(2):
                f = 2 * a + b
                tile = x[b * 128 : (b + 1) * 128]

                @pl.when(f == feat)
                def _():
                    own[j] = tile

                @pl.when(f != feat)
                def _():
                    stage[j, f] = tile.astype(BF16)
                    send(stage.at[j, f], rs.at[j, feat], rs_out.at[j], rs_in.at[j], (tok, f))

    def add_up(j):
        wait(rs.at[j, 0:7], rs_in.at[j])
        total[j] = own[j]

        @pl.loop(1, 8)
        def _(p):
            total[j] += rs[j, feat_peer(p)].astype(F32)

    def fold(v):
        v = jnp.sum(v.reshape(16, 8, 256), axis=0)
        return v[:, :128] + v[:, 128:]

    def norms(s):
        k, l = total[s], total[5 + s]
        weight = 2.0 if s in (1, 2, 3) else 1.0
        for i, v in enumerate((k * l, k * k, l * l)):
            v = weight * fold(v)
            if s:
                red[0, i] += v
            else:
                red[0, i] = v

    launch(T, 0)
    launch(S, 1)
    for s in range(5):
        relay(T, s)
        have(T, s)
        partials(T, s, s)
        relay(S, s)
        have(S, s)
        partials(S, s, 5 + s)
        if s:
            add_up(s - 1)
            add_up(5 + s - 1)
            norms(s - 1)
    add_up(4)
    add_up(9)
    norms(4)

    groups = (
        [(tok, feat_peer(p)) for p in range(1, 8)],
        [(tok_of(xl, z + p, core), feat) for p in range(1, 8)],
        [x_other, sibling, (tok_of(1 - xl, z, 1 - core), feat)],
    )
    for g, peers in enumerate(groups):
        n = len(peers)
        for i, device in enumerate(peers):
            send(red.at[g], redr.at[g, i], red_out.at[g], red_in.at[g], device)
        wait(redr.at[g, 0:n], red_in.at[g])
        v = red[g]
        for i in range(n):
            v = v + redr[g, i]
        red[g + 1] = v

    cross = jnp.sum(red[3, 0], axis=(0, 1), keepdims=True)
    knorm = jnp.sqrt(jnp.sum(red[3, 1], axis=(0, 1), keepdims=True))
    lnorm = jnp.sqrt(jnp.sum(red[3, 2], axis=(0, 1), keepdims=True))
    loss_ref[...] = -cross / (knorm * lnorm)
    by_kern = -1.0 / (knorm * lnorm)
    by_lern = cross / (knorm * lnorm * lnorm * lnorm)

    def weights(s):
        return by_kern * total[s] + by_lern * total[5 + s]

    for s in (1, 2, 3):
        w = weights(s)
        wn[feat, :, s * 256 : (s + 1) * 256] = w.astype(BF16)
        theirs = (core * 2 + lax.rem(y, 2)) * 2 + y // 2
        for side in range(2):
            i = 2 * (s - 1) + side
            tst[i] = jnp.transpose(w[:, side * 128 : (side + 1) * 128]).astype(BF16)
            to = (tok_of(1 - xl, z - s, xh), swapped) if side else (tok_of(xl, z + s, xh), swapped)
            send(tst.at[i], wt.at[theirs, :, i * 128 : (i + 1) * 128], tr_out.at[0], tr_in.at[0], to)
    for s in (0, 4):
        wn[feat, :, s * 256 : (s + 1) * 256] = weights(s).astype(BF16)
    for p in range(1, 8):
        send(wn.at[feat], wn.at[feat], agn_out.at[0], agn_in.at[feat], (tok, feat_peer(p)))
    relay(S, 5)

    def mine_t(f):
        return ((f // 4) * 2 + lax.rem(f, 2)) * 2 + lax.rem(f, 4) // 2

    me_t = mine_t(feat)
    wait(wt.at[me_t], tr_in.at[0])
    for p in range(1, 8):
        send(wt.at[me_t], wt.at[me_t], agt_out.at[0], agt_in.at[me_t], (tok, feat_peer(p)))
    relay(S, 6)
    relay(S, 7)

    acc[...] = jnp.zeros_like(acc)

    def pair(buf, sem, mine, a):
        for b in range(2):
            f = 2 * a + b

            @pl.when(f != mine)
            def _():
                wait(buf.at[f], sem.at[f])

    @pl.loop(0, 4)
    def _(p):
        a = lax.rem(feat // 2 + p, 4)
        pair(wn, agn_in, feat, a)
        w = wn[pl.ds(2 * a, 2)].reshape(256, 1280)
        acc[...] += jnp.dot(w, sb[a, 0:5].reshape(1280, 640), preferred_element_type=F32)

    for k in (5, 6, 7):
        have(S, k)

    @pl.loop(0, 4)
    def _(p):
        a = lax.rem(me_t // 2 + p, 4)
        pair(wt, agt_in, me_t, a)
        w = wt[pl.ds(2 * a, 2)].reshape(256, 768)
        acc[...] += jnp.dot(w, sb[a, 5:8].reshape(768, 640), preferred_element_type=F32)

    grad_ref[...] = (2.0 * TOKENS * DS) * acc[...]

    for kind, index in ((T, 0), (S, 1)):
        src, buf, ring, cores, ring_out, core_out, last = kind
        wait(src, x_out.at[index])
        for k in range(last):
            wait(buf.at[0:2, 0] if k else buf.at[0:2, 0], ring_out.at[k])
        for k in range(last + 1):
            wait(buf.at[0:2, 0], core_out.at[k])
    for j in range(10):
        wait(rs.at[j, 0:7], rs_out.at[j])
    for g, peers in enumerate(groups):
        wait(redr.at[g, 0 : len(peers)], red_out.at[g])
    wait(wt.at[0], tr_out.at[0])
    wait(wn.at[0:7], agn_out.at[0])
    wait(wt.at[0:7], agt_out.at[0])


def local(teacher, student):
    rows, dt = teacher.shape
    ds = student.shape[1]
    dma = pltpu.SemaphoreType.DMA
    loss, grad = pl.pallas_call(
        kernel,
        out_shape=(jax.ShapeDtypeStruct((1, 1), F32), jax.ShapeDtypeStruct((rows, ds), F32)),
        in_specs=[pl.BlockSpec(memory_space=pltpu.VMEM)] * 2,
        out_specs=[pl.BlockSpec(memory_space=pltpu.VMEM)] * 2,
        scratch_shapes=[
            pltpu.VMEM((4, 5, 2, 128, dt), BF16),
            pltpu.VMEM((4, 8, 2, 128, ds), BF16),
            pltpu.VMEM((10, 8, 128, 256), BF16),
            pltpu.VMEM((10, 8, 128, 256), BF16),
            pltpu.VMEM((10, 128, 256), F32),
            pltpu.VMEM((10, 128, 256), F32),
            pltpu.VMEM((8, 128, 1280), BF16),
            pltpu.VMEM((8, 128, 768), BF16),
            pltpu.VMEM((6, 128, 128), BF16),
            pltpu.VMEM((4, 3, 8, 128), F32),
            pltpu.VMEM((3, 7, 3, 8, 128), F32),
            pltpu.VMEM((rows, ds), F32),
            dma((5, 2, 2)), dma((5,)), dma((4,)), dma((5,)),
            dma((8, 2, 2)), dma((8,)), dma((7,)), dma((8,)), dma((2,)),
            dma((10,)), dma((10,)), dma((3,)), dma((3,)), dma((1,)), dma((1,)),
            dma((8,)), dma((1,)), dma((8,)), dma((1,)),
        ],
        compiler_params=pltpu.CompilerParams(
            collective_id=0, has_side_effects=True, vmem_limit_bytes=60 * 2**20
        ),
        cost_estimate=pl.CostEstimate(flops=7 * 10**9, bytes_accessed=2 * 10**6, transcendentals=0),
    )(teacher, student)
    return loss.reshape(()), grad


def solution(mesh):
    placed = (P("tok", "feat"), P("tok", "feat"))
    return jax.shard_map(
        local, mesh=mesh, in_specs=placed, out_specs=(P(), P("tok", "feat")), check_vma=False
    )
```

```python
import functools

import jax
import jax.numpy as jnp
from jax import lax
from jax.experimental import pallas as pl
from jax.experimental.pallas import tpu as pltpu
from jax.sharding import PartitionSpec as P

TOKENS = 8192
DS = 5120
MESH = pl.DeviceIdType.MESH
F32 = jnp.float32
BF16 = jnp.bfloat16


def slot(k):
    return k if k <= 4 else 12 - k


def kernel(
    t_ref, s_ref, loss_ref, grad_ref,
    tb, sb, stage, rs, own, total, wn, wt, tst, red, redr, acc,
    t_ring, t_core, t_ring_out, t_core_out,
    s_ring, s_core, s_ring_out, s_core_out, x_out,
    rs_in, rs_out, red_in, red_out, tr_in, tr_out, agn_in, agn_out, agt_in, agt_out,
):
    tok = lax.axis_index("tok")
    feat = lax.axis_index("feat")
    core = lax.rem(tok, 2)
    z = lax.rem(tok // 2, 8)
    xl = tok // 16
    y = lax.rem(feat, 4)
    xh = feat // 4

    def tok_of(x_lo, zz, c):
        return (x_lo * 8 + lax.rem(zz + 16, 8)) * 2 + c

    z_down = (tok_of(xl, z - 1, core), feat)
    z_up = (tok_of(xl, z + 1, core), feat)
    x_other = (tok_of(1 - xl, z, core), feat)
    sibling = (tok_of(xl, z, 1 - core), feat)

    def feat_peer(p):
        return lax.rem(feat + p, 8)

    swapped = core * 4 + y

    barrier = pltpu.get_barrier_semaphore()

    def greet(device):
        pl.semaphore_signal(barrier, inc=1, device_id=device, device_id_type=MESH)

    for p in range(1, 8):
        greet((tok, feat_peer(p)))
        greet((tok_of(xl, z + p, core), feat))
    for device in (x_other, sibling, (tok_of(1 - xl, z, 1 - core), feat)):
        greet(device)
    for s in (1, 2, 3):
        for sign in (s, -s):
            greet((tok_of(xl, z + sign, xh), swapped))
            greet((tok_of(1 - xl, z + sign, xh), swapped))
    pl.semaphore_wait(barrier, 29)

    def send(src, dst, out_sem, in_sem, device):
        pltpu.make_async_remote_copy(
            src_ref=src, dst_ref=dst, send_sem=out_sem, recv_sem=in_sem, device_id=device, device_id_type=MESH
        ).start()

    def wait(ref, sem):
        pltpu.make_async_copy(ref, ref, sem).wait()

    T = (t_ref, tb, t_ring, t_core, t_ring_out, t_core_out, 4)
    S = (s_ref, sb, s_ring, s_core, s_ring_out, s_core_out, 7)

    def launch(kind, index):
        src, buf, ring, cores, ring_out, core_out, last = kind
        for h in range(2):
            a = 2 * core + h
            rows = src.at[h * 128 : (h + 1) * 128]
            send(rows, buf.at[a, 0, 1], x_out.at[index], ring.at[0, 1, h], x_other)
            send(rows, buf.at[a, 1, 0], ring_out.at[0], ring.at[1, 0, h], z_down)
        for h in range(2):
            a = 2 * core + h
            rows = src.at[h * 128 : (h + 1) * 128]
            send(rows, buf.at[a, 0, 0], core_out.at[0], cores.at[0, h], sibling)
            buf[a, 0, 0] = src[h * 128 : (h + 1) * 128]

    def relay(kind, k, h):
        src, buf, ring, cores, ring_out, core_out, last = kind
        here, there = slot(k), slot(k + 1)
        a = 2 * core + h
        for side in (0, 1) if k else (1,):
            block = buf.at[a, here, side]
            wait(block, ring.at[here, side, h])
            if k < last:
                to = z_up if side else z_down
                send(block, buf.at[a, there, side], ring_out.at[k], ring.at[there, side, h], to)
            send(block, block, core_out.at[here], cores.at[here, h], sibling)

    def have(kind, k, h):
        wait(kind[1].at[0, slot(k)], kind[3].at[slot(k), h])

    def partials(kind, s, j, h):
        src, buf = kind[0], kind[1]

        @pl.loop(0, 2)
        def _(p):
            a = 2 * lax.rem(core + p, 2) + h

            @pl.when(p == 1)
            def _():
                have(kind, s, h)

            rows = buf[a, s].reshape(256, src.shape[1])
            x = lax.dot_general(src[...], rows, (((1,), (1,)), ((), ())), preferred_element_type=F32)
            for b in range(2):
                f = (a // 2) * 4 + lax.rem(a, 2) + 2 * b
                tile = x[b * 128 : (b + 1) * 128]

                @pl.when(f == feat)
                def _():
                    own[j] = tile

                @pl.when(f != feat)
                def _():
                    stage[j, f] = tile.astype(BF16)
                    send(stage.at[j, f], rs.at[j, feat], rs_out.at[j], rs_in.at[j], (tok, f))

    def add_up(j):
        wait(rs.at[j, 0:7], rs_in.at[j])
        total[j] = own[j]

        @pl.loop(1, 8)
        def _(p):
            total[j] += rs[j, feat_peer(p)].astype(F32)

    def fold(v):
        v = jnp.sum(v.reshape(16, 8, 256), axis=0)
        return v[:, :128] + v[:, 128:]

    def norms(s):
        k, l = total[s], total[5 + s]
        weight = 2.0 if s in (1, 2, 3) else 1.0
        for i, v in enumerate((k * l, k * k, l * l)):
            v = weight * fold(v)
            if s:
                red[0, i] += v
            else:
                red[0, i] = v

    launch(S, 0)
    launch(T, 1)
    for s in range(5):
        for kind, j in ((S, 5 + s), (T, s)):
            for h in range(2):
                relay(kind, s, h)
                partials(kind, s, j, h)
        if s:
            add_up(s - 1)
            add_up(5 + s - 1)
            norms(s - 1)
    add_up(4)
    add_up(9)
    norms(4)

    groups = (
        [(tok, feat_peer(p)) for p in range(1, 8)],
        [(tok_of(xl, z + p, core), feat) for p in range(1, 8)],
        [x_other, sibling, (tok_of(1 - xl, z, 1 - core), feat)],
    )
    for g, peers in enumerate(groups):
        n = len(peers)
        for i, device in enumerate(peers):
            send(red.at[g], redr.at[g, i], red_out.at[g], red_in.at[g], device)
        wait(redr.at[g, 0:n], red_in.at[g])
        v = red[g]
        for i in range(n):
            v = v + redr[g, i]
        red[g + 1] = v

    cross = jnp.sum(red[3, 0], axis=(0, 1), keepdims=True)
    knorm = jnp.sqrt(jnp.sum(red[3, 1], axis=(0, 1), keepdims=True))
    lnorm = jnp.sqrt(jnp.sum(red[3, 2], axis=(0, 1), keepdims=True))
    loss_ref[...] = -cross / (knorm * lnorm)
    by_kern = -1.0 / (knorm * lnorm)
    by_lern = cross / (knorm * lnorm * lnorm * lnorm)

    def weights(s):
        return by_kern * total[s] + by_lern * total[5 + s]

    def tile_of(f):
        return ((f // 4) * 2 + lax.rem(f, 2)) * 2 + lax.rem(f, 4) // 2

    here = tile_of(feat)
    for s in (1, 2, 3):
        w = weights(s)
        wn[here, :, s * 256 : (s + 1) * 256] = w.astype(BF16)
        for side in range(2):
            i = 2 * (s - 1) + side
            tst[i] = jnp.transpose(w[:, side * 128 : (side + 1) * 128]).astype(BF16)
            to = (tok_of(1 - xl, z - s, xh), swapped) if side else (tok_of(xl, z + s, xh), swapped)
            send(tst.at[i], wt.at[swapped, :, i * 128 : (i + 1) * 128], tr_out.at[0], tr_in.at[0], to)
    for s in (0, 4):
        wn[here, :, s * 256 : (s + 1) * 256] = weights(s).astype(BF16)

    up = xh * 4 + lax.rem(y + 1, 4)
    down = xh * 4 + lax.rem(y + 3, 4)
    far = xh * 4 + lax.rem(y + 2, 4)

    def across(f):
        return lax.rem(f + 4, 8)

    N = (wn, tile_of, agn_out, agn_in)
    R = (wt, lambda f: f, agt_out, agt_in)

    def give(group, f, part, to, i):
        buf, place, out, into = group
        ref = buf.at[place(f)]
        if part is not None:
            ref = ref.at[part * 64 : (part + 1) * 64]
        send(ref, ref, out.at[0], into.at[i], (tok, to))

    def got(group, f, part, i):
        buf, place, out, into = group
        ref = buf.at[place(f)]
        if part is not None:
            ref = ref.at[part * 64 : (part + 1) * 64]
        wait(ref, into.at[i])

    def first(group):
        give(group, feat, None, up, 0)
        give(group, feat, None, down, 1)
        give(group, feat, None, across(feat), 2)

    def second(group):
        got(group, down, None, 0)
        give(group, down, 0, up, 3)
        got(group, up, None, 1)
        give(group, up, 1, down, 4)
        got(group, across(feat), None, 2)
        give(group, across(feat), None, up, 5)
        give(group, across(feat), None, down, 6)

    def third(group):
        for part in range(2):
            got(group, far, part, 3 + part)
            give(group, far, part, across(feat), 7 + part)

    def fourth(group):
        got(group, across(down), None, 5)
        got(group, across(up), None, 6)
        for part in range(2):
            got(group, across(far), part, 7 + part)

    def product(buf, plane, lo, hi):
        @pl.loop(0, 2)
        def _(p):
            a = 2 * plane + p
            depth = (hi - lo) * 256
            w = buf[pl.ds(2 * a, 2)].reshape(256, depth)
            acc[...] += jnp.dot(w, sb[a, lo:hi].reshape(depth, DS // 8), preferred_element_type=F32)

    first(N)
    for h in range(2):
        relay(S, 5, h)
    wait(wt.at[feat], tr_in.at[0])
    first(R)
    second(N)
    for h in range(2):
        relay(S, 6, h)
    second(R)
    third(N)
    for h in range(2):
        relay(S, 7, h)
    third(R)
    acc[...] = jnp.zeros_like(acc)
    product(wn, xh, 0, 5)
    for k in (5, 6, 7):
        for h in range(2):
            have(S, k, h)
    product(wt, xh, 5, 8)
    fourth(N)
    product(wn, 1 - xh, 0, 5)
    fourth(R)
    product(wt, 1 - xh, 5, 8)

    grad_ref[...] = (2.0 * TOKENS * DS) * acc[...]

    for kind, index in ((S, 0), (T, 1)):
        src, buf, ring, cores, ring_out, core_out, last = kind
        wait(src, x_out.at[index])
        for k in range(last):
            wait(buf.at[0:2, 0], ring_out.at[k])
        for k in range(last + 1):
            wait(buf.at[0:2, 0], core_out.at[k])
    for j in range(10):
        wait(rs.at[j, 0:7], rs_out.at[j])
    for g, peers in enumerate(groups):
        wait(redr.at[g, 0 : len(peers)], red_out.at[g])
    wait(wt.at[0], tr_out.at[0])
    wait(wn.at[0:7], agn_out.at[0])
    wait(wt.at[0:7], agt_out.at[0])


def local(teacher, student):
    rows, dt = teacher.shape
    ds = student.shape[1]
    dma = pltpu.SemaphoreType.DMA
    loss, grad = pl.pallas_call(
        kernel,
        out_shape=(jax.ShapeDtypeStruct((1, 1), F32), jax.ShapeDtypeStruct((rows, ds), F32)),
        in_specs=[pl.BlockSpec(memory_space=pltpu.VMEM)] * 2,
        out_specs=[pl.BlockSpec(memory_space=pltpu.VMEM)] * 2,
        scratch_shapes=[
            pltpu.VMEM((4, 5, 2, 128, dt), BF16),
            pltpu.VMEM((4, 8, 2, 128, ds), BF16),
            pltpu.VMEM((10, 8, 128, 256), BF16),
            pltpu.VMEM((10, 8, 128, 256), BF16),
            pltpu.VMEM((10, 128, 256), F32),
            pltpu.VMEM((10, 128, 256), F32),
            pltpu.VMEM((8, 128, 1280), BF16),
            pltpu.VMEM((8, 128, 768), BF16),
            pltpu.VMEM((6, 128, 128), BF16),
            pltpu.VMEM((4, 3, 8, 128), F32),
            pltpu.VMEM((3, 7, 3, 8, 128), F32),
            pltpu.VMEM((rows, ds), F32),
            dma((5, 2, 2)), dma((5, 2)), dma((4,)), dma((5,)),
            dma((8, 2, 2)), dma((8, 2)), dma((7,)), dma((8,)), dma((2,)),
            dma((10,)), dma((10,)), dma((3,)), dma((3,)), dma((1,)), dma((1,)),
            dma((9,)), dma((1,)), dma((9,)), dma((1,)),
        ],
        compiler_params=pltpu.CompilerParams(
            collective_id=0, has_side_effects=True, vmem_limit_bytes=60 * 2**20
        ),
        cost_estimate=pl.CostEstimate(flops=7 * 10**9, bytes_accessed=2 * 10**6, transcendentals=0),
    )(teacher, student)
    return loss.reshape(()), grad


def solution(mesh):
    placed = (P("tok", "feat"), P("tok", "feat"))
    return jax.shard_map(
        local, mesh=mesh, in_specs=placed, out_specs=(P(), P("tok", "feat")), check_vma=False
    )
```

```python
import functools

import jax
import jax.numpy as jnp
from jax import lax
from jax.experimental import pallas as pl
from jax.experimental.pallas import tpu as pltpu
from jax.sharding import PartitionSpec as P

TOKENS = 8192
DS = 5120
MESH = pl.DeviceIdType.MESH
F32 = jnp.float32
BF16 = jnp.bfloat16


def slot(k):
    return k if k <= 4 else 12 - k


def kernel(
    t_ref, s_ref, loss_ref, grad_ref,
    tb, sb, stage, rs, own, total, wn, wt, tst, red, redr, acc,
    t_ring, t_core, t_ring_out, t_core_out,
    s_ring, s_core, s_ring_out, s_core_out, x_out,
    rs_in, rs_out, red_in, red_out, tr_in, tr_out, agn_in, agn_out, agt_in, agt_out,
):
    tok = lax.axis_index("tok")
    feat = lax.axis_index("feat")
    core = lax.rem(tok, 2)
    z = lax.rem(tok // 2, 8)
    xl = tok // 16
    y = lax.rem(feat, 4)
    xh = feat // 4

    def tok_of(x_lo, zz, c):
        return (x_lo * 8 + lax.rem(zz + 16, 8)) * 2 + c

    z_down = (tok_of(xl, z - 1, core), feat)
    z_up = (tok_of(xl, z + 1, core), feat)
    x_other = (tok_of(1 - xl, z, core), feat)
    sibling = (tok_of(xl, z, 1 - core), feat)

    def feat_peer(p):
        return lax.rem(feat + p, 8)

    swapped = core * 4 + y

    barrier = pltpu.get_barrier_semaphore()

    def greet(device):
        pl.semaphore_signal(barrier, inc=1, device_id=device, device_id_type=MESH)

    for p in range(1, 8):
        greet((tok, feat_peer(p)))
    for device in (z_down, z_up, x_other, sibling):
        greet(device)
    pl.semaphore_wait(barrier, 11)

    def send(src, dst, out_sem, in_sem, device):
        pltpu.make_async_remote_copy(
            src_ref=src, dst_ref=dst, send_sem=out_sem, recv_sem=in_sem, device_id=device, device_id_type=MESH
        ).start()

    def wait(ref, sem):
        pltpu.make_async_copy(ref, ref, sem).wait()

    T = (t_ref, tb, t_ring, t_core, t_ring_out, t_core_out, 4)
    S = (s_ref, sb, s_ring, s_core, s_ring_out, s_core_out, 7)

    def launch(kind, index):
        src, buf, ring, cores, ring_out, core_out, last = kind
        for h in range(2):
            a = 2 * core + h
            rows = src.at[h * 128 : (h + 1) * 128]
            send(rows, buf.at[a, 0, 1], x_out.at[index], ring.at[0, 1, h], x_other)
            send(rows, buf.at[a, 1, 0], ring_out.at[0], ring.at[1, 0, h], z_down)
        for h in range(2):
            a = 2 * core + h
            rows = src.at[h * 128 : (h + 1) * 128]
            send(rows, buf.at[a, 0, 0], core_out.at[0], cores.at[0, h], sibling)
            buf[a, 0, 0] = src[h * 128 : (h + 1) * 128]

    def relay(kind, k, h, sides=(0, 1)):
        src, buf, ring, cores, ring_out, core_out, last = kind
        here, there = slot(k), slot(k + 1)
        a = 2 * core + h
        for side in sides if k else (1,):
            block = buf.at[a, here, side]
            wait(block, ring.at[here, side, h])
            send(block, block, core_out.at[here], cores.at[here, h], sibling)
            if k < last and k != 4:
                to = z_up if side else z_down
                send(block, buf.at[a, there, side], ring_out.at[k], ring.at[there, side, h], to)

    def pass_on(kind, k):
        src, buf, ring, cores, ring_out, core_out, last = kind
        here, there = slot(k), slot(k + 1)
        for h in range(2):
            for side in range(2):
                a = 2 * core + h
                to = z_up if side else z_down
                send(buf.at[a, here, side], buf.at[a, there, side], ring_out.at[k], ring.at[there, side, h], to)

    def have(kind, k, h):
        wait(kind[1].at[0, slot(k)], kind[3].at[slot(k), h])

    def partials(kind, s, j, h):
        src, buf = kind[0], kind[1]

        @pl.loop(0, 2)
        def _(p):
            a = 2 * lax.rem(core + p, 2) + h

            @pl.when(p == 1)
            def _():
                have(kind, s, h)

            rows = buf[a, s].reshape(256, src.shape[1])
            x = lax.dot_general(src[...], rows, (((1,), (1,)), ((), ())), preferred_element_type=F32)
            for b in range(2):
                f = (a // 2) * 4 + lax.rem(a, 2) + 2 * b
                tile = x[b * 128 : (b + 1) * 128]

                @pl.when(f == feat)
                def _():
                    own[j] = tile

                @pl.when(f != feat)
                def _():
                    stage[j, f] = tile.astype(BF16)
                    send(stage.at[j, f], rs.at[j, feat], rs_out.at[j], rs_in.at[j], (tok, f))

    def add_up(j):
        wait(rs.at[j, 0:7], rs_in.at[j])

        @pl.loop(0, 4)
        def _(i):
            rows = pl.ds(pl.multiple_of(i * 32, 32), 32)
            v = own[j, rows]
            for p in range(1, 8):
                v = v + rs[j, feat_peer(p), rows].astype(F32)
            total[j, rows] = v

    def norms(s):
        k, l = total[s], total[5 + s]
        weight = 2.0 if s in (1, 2, 3) else 1.0
        for i, v in enumerate((k * l, k * k, l * l)):
            v = weight * jnp.sum(v, axis=0, keepdims=True)
            red[0, i : i + 1] += v[:, :128] + v[:, 128:]

    def step_sums(s):
        add_up(5 + s)
        add_up(s)
        norms(s)

    launch(S, 0)
    launch(T, 1)
    red[0] = jnp.zeros((8, 128), F32)
    for s in range(5):
        for kind, j in ((S, 5 + s), (T, s)):
            early = False
            for h in range(2) if early else ():
                relay(kind, s, h, (0,))
            for h in range(2):
                relay(kind, s, h, (1,) if early else (0, 1))
                if kind is T and s == 4 and h == 1:
                    pass_on(S, 4)
                partials(kind, s, j, h)
            if kind is S and s:
                step_sums(s - 1)
    step_sums(4)

    def tok_at(p, q):
        return tok_of(lax.rem(xl + p, 2), z, core), feat_peer(q)

    groups = (
        [tok_at(p, q) for p in range(2) for q in range(8) if p or q],
        [(tok_of(xl, z + p, lax.rem(core + q, 2)), feat) for q in range(2) for p in range(8) if p or q],
    )
    for g, peers in enumerate(groups):
        for i, device in enumerate(peers):
            send(red.at[g], redr.at[g, i], red_out.at[g], red_in.at[g], device)
        for h in range(2):
            relay(S, 5 + g, h)
        wait(redr.at[g], red_in.at[g])
        v = red[g]
        for i in range(15):
            v = v + redr[g, i]
        red[g + 1] = v

    cross, ksq, lsq = (jnp.sum(red[2, i : i + 1], axis=1, keepdims=True) for i in range(3))
    knorm = jnp.sqrt(ksq)
    lnorm = jnp.sqrt(lsq)
    loss_ref[...] = -cross / (knorm * lnorm)
    by_kern = -1.0 / (knorm * lnorm)
    by_lern = cross / (knorm * lnorm * lnorm * lnorm)

    def weights(s):
        return by_kern * total[s] + by_lern * total[5 + s]

    def tile_of(f):
        return ((f // 4) * 2 + lax.rem(f, 2)) * 2 + lax.rem(f, 4) // 2

    here = tile_of(feat)
    for s in (1, 2, 3):
        w = weights(s)
        wn[here, :, s * 256 : (s + 1) * 256] = w.astype(BF16)
        for side in range(2):
            i = 2 * (s - 1) + side
            tst[i] = jnp.transpose(w[:, side * 128 : (side + 1) * 128]).astype(BF16)
            to = (tok_of(1 - xl, z - s, xh), swapped) if side else (tok_of(xl, z + s, xh), swapped)
            send(tst.at[i], wt.at[swapped, :, i * 128 : (i + 1) * 128], tr_out.at[0], tr_in.at[0], to)
    for s in (0, 4):
        wn[here, :, s * 256 : (s + 1) * 256] = weights(s).astype(BF16)

    up = xh * 4 + lax.rem(y + 1, 4)
    down = xh * 4 + lax.rem(y + 3, 4)
    far = xh * 4 + lax.rem(y + 2, 4)

    def across(f):
        return lax.rem(f + 4, 8)

    N = (wn, tile_of, agn_out, agn_in)
    R = (wt, lambda f: f, agt_out, agt_in)

    def give(group, f, part, to, i):
        buf, place, out, into = group
        ref = buf.at[place(f)]
        if part is not None:
            ref = ref.at[part * 64 : (part + 1) * 64]
        send(ref, ref, out.at[0], into.at[i], (tok, to))

    def got(group, f, part, i):
        buf, place, out, into = group
        ref = buf.at[place(f)]
        if part is not None:
            ref = ref.at[part * 64 : (part + 1) * 64]
        wait(ref, into.at[i])

    def first(group):
        give(group, feat, None, up, 0)
        give(group, feat, None, down, 1)
        give(group, feat, None, across(feat), 2)

    def second(group):
        got(group, down, None, 0)
        give(group, down, 0, up, 3)
        got(group, up, None, 1)
        give(group, up, 1, down, 4)
        got(group, across(feat), None, 2)
        give(group, across(feat), None, up, 5)
        give(group, across(feat), None, down, 6)

    def third(group):
        for part in range(2):
            got(group, far, part, 3 + part)
            give(group, far, part, across(feat), 7 + part)

    def fourth(group):
        got(group, across(down), None, 5)
        got(group, across(up), None, 6)
        for part in range(2):
            got(group, across(far), part, 7 + part)

    def product(buf, plane, lo, hi):
        @pl.loop(0, 2)
        def _(p):
            a = 2 * plane + p
            depth = (hi - lo) * 256
            w = buf[pl.ds(2 * a, 2)].reshape(256, depth)
            acc[...] += jnp.dot(w, sb[a, lo:hi].reshape(depth, DS // 8), preferred_element_type=F32)

    first(N)
    wait(wt.at[feat], tr_in.at[0])
    first(R)
    second(N)
    for h in range(2):
        relay(S, 7, h)
    second(R)
    third(N)
    third(R)
    acc[...] = jnp.zeros_like(acc)
    product(wn, xh, 0, 5)
    for k in (5, 6, 7):
        for h in range(2):
            have(S, k, h)
    product(wt, xh, 5, 8)
    fourth(N)
    product(wn, 1 - xh, 0, 5)
    fourth(R)
    product(wt, 1 - xh, 5, 8)

    grad_ref[...] = (2.0 * TOKENS * DS) * acc[...]

    for kind, index in ((S, 0), (T, 1)):
        src, buf, ring, cores, ring_out, core_out, last = kind
        wait(src, x_out.at[index])
        for k in range(last):
            wait(buf.at[0:2, 0], ring_out.at[k])
        for k in range(last + 1):
            wait(buf.at[0:2, 0], core_out.at[k])
    for j in range(10):
        wait(rs.at[j, 0:7], rs_out.at[j])
    for g, peers in enumerate(groups):
        wait(redr.at[g], red_out.at[g])
    wait(wt.at[0], tr_out.at[0])
    wait(wn.at[0:7], agn_out.at[0])
    wait(wt.at[0:7], agt_out.at[0])


def local(teacher, student):
    rows, dt = teacher.shape
    ds = student.shape[1]
    dma = pltpu.SemaphoreType.DMA
    loss, grad = pl.pallas_call(
        kernel,
        out_shape=(jax.ShapeDtypeStruct((1, 1), F32), jax.ShapeDtypeStruct((rows, ds), F32)),
        in_specs=[pl.BlockSpec(memory_space=pltpu.VMEM)] * 2,
        out_specs=[pl.BlockSpec(memory_space=pltpu.VMEM)] * 2,
        scratch_shapes=[
            pltpu.VMEM((4, 5, 2, 128, dt), BF16),
            pltpu.VMEM((4, 8, 2, 128, ds), BF16),
            pltpu.VMEM((10, 8, 128, 256), BF16),
            pltpu.VMEM((10, 8, 128, 256), BF16),
            pltpu.VMEM((10, 128, 256), F32),
            pltpu.VMEM((10, 128, 256), F32),
            pltpu.VMEM((8, 128, 1280), BF16),
            pltpu.VMEM((8, 128, 768), BF16),
            pltpu.VMEM((6, 128, 128), BF16),
            pltpu.VMEM((3, 8, 128), F32),
            pltpu.VMEM((2, 15, 8, 128), F32),
            pltpu.VMEM((rows, ds), F32),
            dma((5, 2, 2)), dma((5, 2)), dma((4,)), dma((5,)),
            dma((8, 2, 2)), dma((8, 2)), dma((7,)), dma((8,)), dma((2,)),
            dma((10,)), dma((10,)), dma((2,)), dma((2,)), dma((1,)), dma((1,)),
            dma((9,)), dma((1,)), dma((9,)), dma((1,)),
        ],
        compiler_params=pltpu.CompilerParams(
            collective_id=0, has_side_effects=True, vmem_limit_bytes=60 * 2**20
        ),
        cost_estimate=pl.CostEstimate(flops=7 * 10**9, bytes_accessed=2 * 10**6, transcendentals=0),
    )(teacher, student)
    return loss.reshape(()), grad


def solution(mesh):
    placed = (P("tok", "feat"), P("tok", "feat"))
    return jax.shard_map(
        local, mesh=mesh, in_specs=placed, out_specs=(P(), P("tok", "feat")), check_vma=False
    )
```

```python
import functools

import jax
import jax.numpy as jnp
from jax import lax
from jax.experimental import pallas as pl
from jax.experimental.pallas import tpu as pltpu
from jax.sharding import PartitionSpec as P

TOKENS = 8192
DS = 5120
MESH = pl.DeviceIdType.MESH
F32 = jnp.float32
HALVES = ((0, 64), (64, 128))
MOST, REST = (0, 112), (112, 128)
BF16 = jnp.bfloat16


def slot(k):
    return k if k <= 4 else 12 - k


def kernel(
    t_hbm, s_hbm, loss_ref, grad_ref, t_ref, s_ref,
    tb, sb, stage, rs, own, total, wn, wt, tst, red, redr,
    t_ring, t_core, t_ring_out, t_core_out,
    s_ring, s_core, s_ring_out, s_core_out, x_out,
    rs_in, rs_out, red_in, red_out, tr_in, tr_out, agn_in, agn_out, agt_in, agt_out, load,
):
    tok = lax.axis_index("tok")
    feat = lax.axis_index("feat")
    core = lax.rem(tok, 2)
    z = lax.rem(tok // 2, 8)
    xl = tok // 16
    y = lax.rem(feat, 4)
    xh = feat // 4

    def tok_of(x_lo, zz, c):
        return (x_lo * 8 + lax.rem(zz + 16, 8)) * 2 + c

    z_down = (tok_of(xl, z - 1, core), feat)
    z_up = (tok_of(xl, z + 1, core), feat)
    x_other = (tok_of(1 - xl, z, core), feat)
    sibling = (tok_of(xl, z, 1 - core), feat)

    def feat_peer(p):
        return lax.rem(feat + p, 8)

    swapped = core * 4 + y

    loads = [pltpu.make_async_copy(a, b, load.at[i]) for i, (a, b) in enumerate(((t_hbm, t_ref), (s_hbm, s_ref)))]
    for copy in loads:
        copy.start()

    barrier = pltpu.get_barrier_semaphore()

    def greet(device):
        pl.semaphore_signal(barrier, inc=1, device_id=device, device_id_type=MESH)

    for p in range(1, 8):
        greet((tok, feat_peer(p)))
    for device in (z_down, z_up, x_other, sibling):
        greet(device)
    pl.semaphore_wait(barrier, 11)
    for copy in loads:
        copy.wait()

    def send(src, dst, out_sem, in_sem, device):
        pltpu.make_async_remote_copy(
            src_ref=src, dst_ref=dst, send_sem=out_sem, recv_sem=in_sem, device_id=device, device_id_type=MESH
        ).start()

    def wait(ref, sem):
        pltpu.make_async_copy(ref, ref, sem).wait()

    T = (t_ref, tb, t_ring, t_core, t_ring_out, t_core_out, 4)
    S = (s_ref, sb, s_ring, s_core, s_ring_out, s_core_out, 7)

    def launch(kind, index):
        src, buf, ring, cores, ring_out, core_out, last = kind
        for h in range(2):
            a = 2 * core + h
            rows = src.at[h * 128 : (h + 1) * 128]
            send(rows, buf.at[a, 0, 1], x_out.at[index], ring.at[0, 1, h], x_other)
            send(rows, buf.at[a, 1, 0], ring_out.at[0], ring.at[1, 0, h], z_down)
        for h in range(2):
            a = 2 * core + h
            rows = src.at[h * 128 : (h + 1) * 128]
            send(rows, buf.at[a, 0, 0], core_out.at[0], cores.at[0, h], sibling)
            buf[a, 0, 0] = src[h * 128 : (h + 1) * 128]

    def relay(kind, k, h, sides=(0, 1)):
        src, buf, ring, cores, ring_out, core_out, last = kind
        here, there = slot(k), slot(k + 1)
        a = 2 * core + h
        for side in sides if k else (1,):
            block = buf.at[a, here, side]
            wait(block, ring.at[here, side, h])
            send(block, block, core_out.at[here], cores.at[here, h], sibling)
            if k < last and k != 4:
                to = z_up if side else z_down
                send(block, buf.at[a, there, side], ring_out.at[k], ring.at[there, side, h], to)

    def pass_on(kind, k):
        src, buf, ring, cores, ring_out, core_out, last = kind
        here, there = slot(k), slot(k + 1)
        for h in range(2):
            for side in range(2):
                a = 2 * core + h
                to = z_up if side else z_down
                send(buf.at[a, here, side], buf.at[a, there, side], ring_out.at[k], ring.at[there, side, h], to)

    def have(kind, k, h):
        wait(kind[1].at[0, slot(k)], kind[3].at[slot(k), h])

    def partials(kind, s, j, h):
        src, buf = kind[0], kind[1]

        @pl.loop(0, 2)
        def _(p):
            a = 2 * lax.rem(core + p, 2) + h

            @pl.when(p == 1)
            def _():
                have(kind, s, h)

            rows = buf[a, s].reshape(256, src.shape[1])
            x = lax.dot_general(src[...], rows, (((1,), (1,)), ((), ())), preferred_element_type=F32)
            for b in range(2):
                f = (a // 2) * 4 + lax.rem(a, 2) + 2 * b
                tile = x[b * 128 : (b + 1) * 128]

                @pl.when(f == feat)
                def _():
                    own[j] = tile

                @pl.when(f != feat)
                def _():
                    stage[j, f] = tile.astype(BF16)
                    send(stage.at[j, f], rs.at[j, feat], rs_out.at[j], rs_in.at[j], (tok, f))

    def add_up(j):
        wait(rs.at[j, 0:7], rs_in.at[j])

        @pl.loop(0, 4)
        def _(i):
            rows = pl.ds(pl.multiple_of(i * 32, 32), 32)
            v = own[j, rows]
            for p in range(1, 8):
                v = v + rs[j, feat_peer(p), rows].astype(F32)
            total[j, rows] = v

    def norms(s):
        k, l = total[s], total[5 + s]
        weight = 2.0 if s in (1, 2, 3) else 1.0
        for i, v in enumerate((k * l, k * k, l * l)):
            v = weight * jnp.sum(v, axis=0, keepdims=True)
            red[0, i : i + 1] += v[:, :128] + v[:, 128:]

    def step_sums(s):
        add_up(5 + s)
        add_up(s)
        norms(s)

    launch(S, 0)
    launch(T, 1)
    red[0] = jnp.zeros((8, 128), F32)
    for s in range(5):
        for kind, j in ((S, 5 + s), (T, s)):
            early = False
            for h in range(2) if early else ():
                relay(kind, s, h, (0,))
            for h in range(2):
                relay(kind, s, h, (1,) if early else (0, 1))
                partials(kind, s, j, h)
                if kind is T and s == 4 and h == 1:
                    pass_on(S, 4)
            if kind is S and s:
                step_sums(s - 1)
    step_sums(4)

    def tok_at(p, q):
        return tok_of(lax.rem(xl + p, 2), z, core), feat_peer(q)

    groups = (
        [tok_at(p, q) for p in range(2) for q in range(8) if p or q],
        [(tok_of(xl, z + p, lax.rem(core + q, 2)), feat) for q in range(2) for p in range(8) if p or q],
    )
    for g, peers in enumerate(groups):
        for i, device in enumerate(peers):
            send(red.at[g], redr.at[g, i], red_out.at[g], red_in.at[g], device)
        wait(redr.at[g], red_in.at[g])
        v = red[g]
        for i in range(15):
            v = v + redr[g, i]
        red[g + 1] = v

    cross, ksq, lsq = (jnp.sum(red[2, i : i + 1], axis=1, keepdims=True) for i in range(3))
    knorm = jnp.sqrt(ksq)
    lnorm = jnp.sqrt(lsq)
    loss_ref[...] = -cross / (knorm * lnorm)
    by_kern = -1.0 / (knorm * lnorm)
    by_lern = cross / (knorm * lnorm * lnorm * lnorm)

    def weights(s):
        return by_kern * total[s] + by_lern * total[5 + s]

    def tile_of(f):
        return ((f // 4) * 2 + lax.rem(f, 2)) * 2 + lax.rem(f, 4) // 2

    here = tile_of(feat)
    for s in (1, 2, 3):
        w = weights(s)
        wn[here, :, s * 256 : (s + 1) * 256] = w.astype(BF16)
        for side in range(2):
            i = 2 * (s - 1) + side
            tst[i] = jnp.transpose(w[:, side * 128 : (side + 1) * 128]).astype(BF16)
            to = (tok_of(1 - xl, z - s, xh), swapped) if side else (tok_of(xl, z + s, xh), swapped)
            send(tst.at[i], wt.at[swapped, :, i * 128 : (i + 1) * 128], tr_out.at[0], tr_in.at[0], to)
    for s in (0, 4):
        wn[here, :, s * 256 : (s + 1) * 256] = weights(s).astype(BF16)

    up = xh * 4 + lax.rem(y + 1, 4)
    down = xh * 4 + lax.rem(y + 3, 4)
    far = xh * 4 + lax.rem(y + 2, 4)

    def across(f):
        return lax.rem(f + 4, 8)

    N = (wn, tile_of, agn_out, agn_in)
    R = (wt, lambda f: f, agt_out, agt_in)

    def give(group, f, part, to, i):
        buf, place, out, into = group
        ref = buf.at[place(f)]
        if part is not None:
            ref = ref.at[part[0] : part[1]]
        send(ref, ref, out.at[0], into.at[i], (tok, to))

    def got(group, f, part, i):
        buf, place, out, into = group
        ref = buf.at[place(f)]
        if part is not None:
            ref = ref.at[part[0] : part[1]]
        wait(ref, into.at[i])

    def first(group):
        give(group, feat, None, across(feat), 2)
        give(group, feat, None, up, 0)
        give(group, feat, None, down, 1)

    def second(group):
        got(group, down, None, 0)
        give(group, down, HALVES[0], up, 3)
        give(group, down, REST, across(feat), 9)
        got(group, up, None, 1)
        give(group, up, HALVES[1], down, 4)
        give(group, up, REST, across(feat), 10)
        got(group, across(feat), None, 2)
        give(group, across(feat), MOST, up, 5)
        give(group, across(feat), MOST, down, 6)

    def third(group):
        for i, part in enumerate(HALVES):
            got(group, far, part, 3 + i)
            give(group, far, part, across(feat), 7 + i)

    def fourth(group):
        got(group, across(down), MOST, 5)
        got(group, across(down), REST, 9)
        got(group, across(up), MOST, 6)
        got(group, across(up), REST, 10)
        for i, part in enumerate(HALVES):
            got(group, across(far), part, 7 + i)

    def product(buf, plane, lo, hi):
        @pl.loop(0, 2)
        def _(p):
            a = 2 * plane + p
            depth = (hi - lo) * 256
            w = buf[pl.ds(2 * a, 2)].reshape(256, depth)
            grad_ref[...] += jnp.dot(w, sb[a, lo:hi].reshape(depth, DS // 8), preferred_element_type=F32)

    first(N)
    wait(wt.at[feat], tr_in.at[0])
    first(R)
    for h in range(2):
        relay(S, 5, h)
    second(N)
    second(R)
    for h in range(2):
        relay(S, 6, h)
    third(N)
    third(R)
    for h in range(2):
        relay(S, 7, h)
    grad_ref[...] = jnp.zeros_like(grad_ref)
    product(wn, xh, 0, 5)
    for k in (5, 6, 7):
        for h in range(2):
            have(S, k, h)
    product(wt, xh, 5, 8)
    fourth(N)
    product(wn, 1 - xh, 0, 5)
    fourth(R)
    product(wt, 1 - xh, 5, 8)

    for kind, index in ((S, 0), (T, 1)):
        src, buf, ring, cores, ring_out, core_out, last = kind
        wait(src, x_out.at[index])
        for k in range(last):
            wait(buf.at[0:2, 0], ring_out.at[k])
        for k in range(last + 1):
            wait(buf.at[0:2, 0], core_out.at[k])
    for j in range(10):
        wait(rs.at[j, 0:7], rs_out.at[j])
    for g, peers in enumerate(groups):
        wait(redr.at[g], red_out.at[g])
    wait(wt.at[0], tr_out.at[0])
    wait(wn.at[0:7], agn_out.at[0])
    wait(wt.at[0:7], agt_out.at[0])


def local(teacher, student):
    rows, dt = teacher.shape
    ds = student.shape[1]
    dma = pltpu.SemaphoreType.DMA
    loss, grad = pl.pallas_call(
        kernel,
        out_shape=(jax.ShapeDtypeStruct((1, 1), F32), jax.ShapeDtypeStruct((rows, ds), F32)),
        in_specs=[pl.BlockSpec(memory_space=pl.ANY)] * 2,
        out_specs=[pl.BlockSpec(memory_space=pltpu.VMEM)] * 2,
        scratch_shapes=[
            pltpu.VMEM((rows, dt), BF16),
            pltpu.VMEM((rows, ds), BF16),
            pltpu.VMEM((4, 5, 2, 128, dt), BF16),
            pltpu.VMEM((4, 8, 2, 128, ds), BF16),
            pltpu.VMEM((10, 8, 128, 256), BF16),
            pltpu.VMEM((10, 8, 128, 256), BF16),
            pltpu.VMEM((10, 128, 256), F32),
            pltpu.VMEM((10, 128, 256), F32),
            pltpu.VMEM((8, 128, 1280), BF16),
            pltpu.VMEM((8, 128, 768), BF16),
            pltpu.VMEM((6, 128, 128), BF16),
            pltpu.VMEM((3, 8, 128), F32),
            pltpu.VMEM((2, 15, 8, 128), F32),
            dma((5, 2, 2)), dma((5, 2)), dma((4,)), dma((5,)),
            dma((8, 2, 2)), dma((8, 2)), dma((7,)), dma((8,)), dma((2,)),
            dma((10,)), dma((10,)), dma((2,)), dma((2,)), dma((1,)), dma((1,)),
            dma((11,)), dma((1,)), dma((11,)), dma((1,)), dma((2,)),
        ],
        compiler_params=pltpu.CompilerParams(
            collective_id=0, has_side_effects=True, vmem_limit_bytes=60 * 2**20
        ),
        cost_estimate=pl.CostEstimate(flops=7 * 10**9, bytes_accessed=2 * 10**6, transcendentals=0),
    )(teacher, student)
    return loss.reshape(()), (2.0 * TOKENS * DS) * grad


def solution(mesh):
    placed = (P("tok", "feat"), P("tok", "feat"))
    return jax.shard_map(
        local, mesh=mesh, in_specs=placed, out_specs=(P(), P("tok", "feat")), check_vma=False
    )
```

```python
import functools

import jax
import jax.numpy as jnp
from jax import lax
from jax.experimental import pallas as pl
from jax.experimental.pallas import tpu as pltpu
from jax.sharding import PartitionSpec as P

TOKENS = 8192
DS = 5120
MESH = pl.DeviceIdType.MESH
F32 = jnp.float32
HALVES = ((0, 64), (64, 128))
MOST, REST = (0, 112), (112, 128)
BF16 = jnp.bfloat16


def slot(k):
    return k if k <= 4 else 12 - k


def kernel(
    t_hbm, s_hbm, loss_ref, grad_ref, t_ref, s_ref,
    tb, sb, stage, rs, own, total, wn, wt, tst, red, redr,
    t_ring, t_core, t_ring_out, t_core_out,
    s_ring, s_core, s_ring_out, s_core_out, x_out,
    rs_in, rs_out, red_in, red_out, tr_in, tr_out, agn_in, agn_out, agt_in, agt_out, load,
):
    tok = lax.axis_index("tok")
    feat = lax.axis_index("feat")
    core = lax.rem(tok, 2)
    z = lax.rem(tok // 2, 8)
    xl = tok // 16
    y = lax.rem(feat, 4)
    xh = feat // 4

    def tok_of(x_lo, zz, c):
        return (x_lo * 8 + lax.rem(zz + 16, 8)) * 2 + c

    z_down = (tok_of(xl, z - 1, core), feat)
    z_up = (tok_of(xl, z + 1, core), feat)
    x_other = (tok_of(1 - xl, z, core), feat)
    sibling = (tok_of(xl, z, 1 - core), feat)

    def feat_peer(p):
        return lax.rem(feat + p, 8)

    swapped = core * 4 + y

    loads = [pltpu.make_async_copy(a, b, load.at[i]) for i, (a, b) in enumerate(((t_hbm, t_ref), (s_hbm, s_ref)))]
    for copy in loads:
        copy.start()

    barrier = pltpu.get_barrier_semaphore()

    def greet(device):
        pl.semaphore_signal(barrier, inc=1, device_id=device, device_id_type=MESH)

    for p in range(1, 8):
        greet((tok, feat_peer(p)))
    for device in (z_down, z_up, x_other, sibling):
        greet(device)
    pl.semaphore_wait(barrier, 11)
    for copy in loads:
        copy.wait()

    def send(src, dst, out_sem, in_sem, device):
        pltpu.make_async_remote_copy(
            src_ref=src, dst_ref=dst, send_sem=out_sem, recv_sem=in_sem, device_id=device, device_id_type=MESH
        ).start()

    def wait(ref, sem):
        pltpu.make_async_copy(ref, ref, sem).wait()

    T = (t_ref, tb, t_ring, t_core, t_ring_out, t_core_out, 4)
    S = (s_ref, sb, s_ring, s_core, s_ring_out, s_core_out, 7)

    def launch(kind, index):
        src, buf, ring, cores, ring_out, core_out, last = kind
        for h in range(2):
            a = 2 * core + h
            rows = src.at[h * 128 : (h + 1) * 128]
            send(rows, buf.at[a, 0, 1], x_out.at[index], ring.at[0, 1, h], x_other)
            send(rows, buf.at[a, 1, 0], ring_out.at[0], ring.at[1, 0, h], z_down)
        for h in range(2):
            a = 2 * core + h
            rows = src.at[h * 128 : (h + 1) * 128]
            send(rows, buf.at[a, 0, 0], core_out.at[0], cores.at[0, h], sibling)
            buf[a, 0, 0] = src[h * 128 : (h + 1) * 128]

    def relay(kind, k, h):
        src, buf, ring, cores, ring_out, core_out, last = kind
        here, there = slot(k), slot(k + 1)
        a = 2 * core + h
        for side in (0, 1) if k else (1,):
            block = buf.at[a, here, side]
            wait(block, ring.at[here, side, h])
            send(block, block, core_out.at[here], cores.at[here, h], sibling)
            if k < last and k != 4:
                to = z_up if side else z_down
                send(block, buf.at[a, there, side], ring_out.at[k], ring.at[there, side, h], to)

    def pass_on(kind, k):
        src, buf, ring, cores, ring_out, core_out, last = kind
        here, there = slot(k), slot(k + 1)
        for h in range(2):
            for side in range(2):
                a = 2 * core + h
                to = z_up if side else z_down
                send(buf.at[a, here, side], buf.at[a, there, side], ring_out.at[k], ring.at[there, side, h], to)

    def have(kind, k, h):
        wait(kind[1].at[0, slot(k)], kind[3].at[slot(k), h])

    def partials(kind, s, j, h):
        src, buf = kind[0], kind[1]

        @pl.loop(0, 2)
        def _(p):
            a = 2 * lax.rem(core + p, 2) + h

            @pl.when(p == 1)
            def _():
                have(kind, s, h)

            rows = buf[a, s].reshape(256, src.shape[1])
            x = lax.dot_general(src[...], rows, (((1,), (1,)), ((), ())), preferred_element_type=F32)
            for b in range(2):
                f = (a // 2) * 4 + lax.rem(a, 2) + 2 * b
                tile = x[b * 128 : (b + 1) * 128]

                @pl.when(f == feat)
                def _():
                    own[j] = tile

                @pl.when(f != feat)
                def _():
                    stage[j, f] = tile.astype(BF16)
                    send(stage.at[j, f], rs.at[j, feat], rs_out.at[j], rs_in.at[j], (tok, f))

    def add_up(j):
        wait(rs.at[j, 0:7], rs_in.at[j])

        @pl.loop(0, 4)
        def _(i):
            rows = pl.ds(pl.multiple_of(i * 32, 32), 32)
            v = own[j, rows]
            for p in range(1, 8):
                v = v + rs[j, feat_peer(p), rows].astype(F32)
            total[j, rows] = v

    def norms(s):
        k, l = total[s], total[5 + s]
        weight = 2.0 if s in (1, 2, 3) else 1.0
        for i, v in enumerate((k * l, k * k, l * l)):
            v = weight * jnp.sum(v, axis=0, keepdims=True)
            red[0, i : i + 1] += v[:, :128] + v[:, 128:]

    def step_sums(s):
        add_up(5 + s)
        add_up(s)
        norms(s)

    launch(S, 0)
    launch(T, 1)
    red[0] = jnp.zeros((8, 128), F32)
    for s in range(5):
        for kind, j in ((S, 5 + s), (T, s)):
            late = kind is T and s == 4
            for h in range(2):
                relay(kind, s, h)
                if late:
                    partials(kind, s, j, h)
            for h in () if late else range(2):
                partials(kind, s, j, h)
            if late:
                pass_on(S, 4)
            if kind is S and s:
                step_sums(s - 1)
    step_sums(4)

    def tok_at(p, q):
        return tok_of(lax.rem(xl + p, 2), z, core), feat_peer(q)

    groups = (
        [tok_at(p, q) for p in range(2) for q in range(8) if p or q],
        [(tok_of(xl, z + p, lax.rem(core + q, 2)), feat) for q in range(2) for p in range(8) if p or q],
    )
    for g, peers in enumerate(groups):
        for i, device in enumerate(peers):
            send(red.at[g], redr.at[g, i], red_out.at[g], red_in.at[g], device)
        wait(redr.at[g], red_in.at[g])
        v = red[g]
        for i in range(15):
            v = v + redr[g, i]
        red[g + 1] = v

    cross, ksq, lsq = (jnp.sum(red[2, i : i + 1], axis=1, keepdims=True) for i in range(3))
    knorm = jnp.sqrt(ksq)
    lnorm = jnp.sqrt(lsq)
    loss_ref[...] = -cross / (knorm * lnorm)
    by_kern = -1.0 / (knorm * lnorm)
    by_lern = cross / (knorm * lnorm * lnorm * lnorm)

    def weights(s):
        return by_kern * total[s] + by_lern * total[5 + s]

    def tile_of(f):
        return ((f // 4) * 2 + lax.rem(f, 2)) * 2 + lax.rem(f, 4) // 2

    here = tile_of(feat)
    for s in (1, 2, 3):
        w = weights(s)
        wn[here, :, s * 256 : (s + 1) * 256] = w.astype(BF16)
        for side in range(2):
            i = 2 * (s - 1) + side
            tst[i] = jnp.transpose(w[:, side * 128 : (side + 1) * 128]).astype(BF16)
            to = (tok_of(1 - xl, z - s, xh), swapped) if side else (tok_of(xl, z + s, xh), swapped)
            send(tst.at[i], wt.at[swapped, :, i * 128 : (i + 1) * 128], tr_out.at[0], tr_in.at[0], to)
    for s in (0, 4):
        wn[here, :, s * 256 : (s + 1) * 256] = weights(s).astype(BF16)

    up = xh * 4 + lax.rem(y + 1, 4)
    down = xh * 4 + lax.rem(y + 3, 4)
    far = xh * 4 + lax.rem(y + 2, 4)

    def across(f):
        return lax.rem(f + 4, 8)

    N = (wn, tile_of, agn_out, agn_in)
    R = (wt, lambda f: f, agt_out, agt_in)

    def give(group, f, part, to, i):
        buf, place, out, into = group
        ref = buf.at[place(f)]
        if part is not None:
            ref = ref.at[part[0] : part[1]]
        send(ref, ref, out.at[0], into.at[i], (tok, to))

    def got(group, f, part, i):
        buf, place, out, into = group
        ref = buf.at[place(f)]
        if part is not None:
            ref = ref.at[part[0] : part[1]]
        wait(ref, into.at[i])

    def first(group):
        give(group, feat, None, across(feat), 2)
        give(group, feat, None, up, 0)
        give(group, feat, None, down, 1)

    def second(group):
        got(group, down, None, 0)
        give(group, down, HALVES[0], up, 3)
        give(group, down, REST, across(feat), 9)
        got(group, up, None, 1)
        give(group, up, HALVES[1], down, 4)
        give(group, up, REST, across(feat), 10)
        got(group, across(feat), None, 2)
        give(group, across(feat), MOST, up, 5)
        give(group, across(feat), MOST, down, 6)

    def third(group):
        for i, part in enumerate(HALVES):
            got(group, far, part, 3 + i)
            give(group, far, part, across(feat), 7 + i)

    def fourth(group):
        got(group, across(down), MOST, 5)
        got(group, across(down), REST, 9)
        got(group, across(up), MOST, 6)
        got(group, across(up), REST, 10)
        for i, part in enumerate(HALVES):
            got(group, across(far), part, 7 + i)

    def product(buf, plane, lo, hi):
        @pl.loop(0, 2)
        def _(p):
            a = 2 * plane + p
            depth = (hi - lo) * 256
            w = buf[pl.ds(2 * a, 2)].reshape(256, depth)
            grad_ref[...] += jnp.dot(w, sb[a, lo:hi].reshape(depth, DS // 8), preferred_element_type=F32)

    first(N)
    wait(wt.at[feat], tr_in.at[0])
    first(R)
    for h in range(2):
        relay(S, 5, h)
    second(N)
    second(R)
    for h in range(2):
        relay(S, 6, h)
    third(N)
    third(R)
    for h in range(2):
        relay(S, 7, h)
    grad_ref[...] = jnp.zeros_like(grad_ref)
    product(wn, xh, 0, 5)
    for k in (5, 6, 7):
        for h in range(2):
            have(S, k, h)
    product(wt, xh, 5, 8)
    fourth(N)
    product(wn, 1 - xh, 0, 5)
    fourth(R)
    product(wt, 1 - xh, 5, 8)

    for kind, index in ((S, 0), (T, 1)):
        src, buf, ring, cores, ring_out, core_out, last = kind
        wait(src, x_out.at[index])
        for k in range(last):
            wait(buf.at[0:2, 0], ring_out.at[k])
        for k in range(last + 1):
            wait(buf.at[0:2, 0], core_out.at[k])
    for j in range(10):
        wait(rs.at[j, 0:7], rs_out.at[j])
    for g, peers in enumerate(groups):
        wait(redr.at[g], red_out.at[g])
    wait(wt.at[0], tr_out.at[0])
    wait(wn.at[0:7], agn_out.at[0])
    wait(wt.at[0:7], agt_out.at[0])


def local(teacher, student):
    rows, dt = teacher.shape
    ds = student.shape[1]
    dma = pltpu.SemaphoreType.DMA
    loss, grad = pl.pallas_call(
        kernel,
        out_shape=(jax.ShapeDtypeStruct((1, 1), F32), jax.ShapeDtypeStruct((rows, ds), F32)),
        in_specs=[pl.BlockSpec(memory_space=pl.ANY)] * 2,
        out_specs=[pl.BlockSpec(memory_space=pltpu.VMEM)] * 2,
        scratch_shapes=[
            pltpu.VMEM((rows, dt), BF16),
            pltpu.VMEM((rows, ds), BF16),
            pltpu.VMEM((4, 5, 2, 128, dt), BF16),
            pltpu.VMEM((4, 8, 2, 128, ds), BF16),
            pltpu.VMEM((10, 8, 128, 256), BF16),
            pltpu.VMEM((10, 8, 128, 256), BF16),
            pltpu.VMEM((10, 128, 256), F32),
            pltpu.VMEM((10, 128, 256), F32),
            pltpu.VMEM((8, 128, 1280), BF16),
            pltpu.VMEM((8, 128, 768), BF16),
            pltpu.VMEM((6, 128, 128), BF16),
            pltpu.VMEM((3, 8, 128), F32),
            pltpu.VMEM((2, 15, 8, 128), F32),
            dma((5, 2, 2)), dma((5, 2)), dma((4,)), dma((5,)),
            dma((8, 2, 2)), dma((8, 2)), dma((7,)), dma((8,)), dma((2,)),
            dma((10,)), dma((10,)), dma((2,)), dma((2,)), dma((1,)), dma((1,)),
            dma((11,)), dma((1,)), dma((11,)), dma((1,)), dma((2,)),
        ],
        compiler_params=pltpu.CompilerParams(
            collective_id=0, has_side_effects=True, vmem_limit_bytes=60 * 2**20
        ),
        cost_estimate=pl.CostEstimate(flops=7 * 10**9, bytes_accessed=2 * 10**6, transcendentals=0),
    )(teacher, student)
    return loss.reshape(()), (2.0 * TOKENS * DS) * grad


def solution(mesh):
    placed = (P("tok", "feat"), P("tok", "feat"))
    return jax.shard_map(
        local, mesh=mesh, in_specs=placed, out_specs=(P(), P("tok", "feat")), check_vma=False
    )
```

```python
import functools

import jax
import jax.numpy as jnp
from jax import lax
from jax.experimental import pallas as pl
from jax.experimental.pallas import tpu as pltpu
from jax.sharding import PartitionSpec as P

TOKENS = 8192
DS = 5120
MESH = pl.DeviceIdType.MESH
F32 = jnp.float32
HALVES = ((0, 64), (64, 128))
MOST, REST = (0, 112), (112, 128)
BF16 = jnp.bfloat16


def slot(k):
    return k if k <= 4 else 12 - k


def kernel(
    t_hbm, s_hbm, loss_ref, grad_ref, t_ref, s_ref,
    tb, sb, stage, rs, own, total, wn, wt, tst, red, redr,
    t_ring, t_core, t_ring_out, t_core_out,
    s_ring, s_core, s_ring_out, s_core_out, x_out,
    rs_in, rs_out, red_in, red_out, tr_in, tr_out, agn_in, agn_out, agt_in, agt_out, load,
):
    tok = lax.axis_index("tok")
    feat = lax.axis_index("feat")
    core = lax.rem(tok, 2)
    z = lax.rem(tok // 2, 8)
    xl = tok // 16
    y = lax.rem(feat, 4)
    xh = feat // 4

    def tok_of(x_lo, zz, c):
        return (x_lo * 8 + lax.rem(zz + 16, 8)) * 2 + c

    z_down = (tok_of(xl, z - 1, core), feat)
    z_up = (tok_of(xl, z + 1, core), feat)
    x_other = (tok_of(1 - xl, z, core), feat)
    sibling = (tok_of(xl, z, 1 - core), feat)

    def feat_peer(p):
        return lax.rem(feat + p, 8)

    swapped = core * 4 + y

    loads = [pltpu.make_async_copy(a, b, load.at[i]) for i, (a, b) in enumerate(((t_hbm, t_ref), (s_hbm, s_ref)))]
    for copy in loads:
        copy.start()

    barrier = pltpu.get_barrier_semaphore()

    def greet(device):
        pl.semaphore_signal(barrier, inc=1, device_id=device, device_id_type=MESH)

    for p in range(1, 8):
        greet((tok, feat_peer(p)))
    for device in (z_down, z_up, x_other, sibling):
        greet(device)
    pl.semaphore_wait(barrier, 11)
    for copy in loads:
        copy.wait()

    def send(src, dst, out_sem, in_sem, device):
        pltpu.make_async_remote_copy(
            src_ref=src, dst_ref=dst, send_sem=out_sem, recv_sem=in_sem, device_id=device, device_id_type=MESH
        ).start()

    def wait(ref, sem):
        pltpu.make_async_copy(ref, ref, sem).wait()

    T = (t_ref, tb, t_ring, t_core, t_ring_out, t_core_out, 4)
    S = (s_ref, sb, s_ring, s_core, s_ring_out, s_core_out, 7)

    def launch(kind, index):
        src, buf, ring, cores, ring_out, core_out, last = kind
        for h in range(2):
            a = 2 * core + h
            rows = src.at[h * 128 : (h + 1) * 128]
            send(rows, buf.at[a, 0, 1], x_out.at[index], ring.at[0, 1, h], x_other)
            send(rows, buf.at[a, 1, 0], ring_out.at[0], ring.at[1, 0, h], z_down)
        for h in range(2):
            a = 2 * core + h
            rows = src.at[h * 128 : (h + 1) * 128]
            send(rows, buf.at[a, 0, 0], core_out.at[0], cores.at[0, h], sibling)
            buf[a, 0, 0] = src[h * 128 : (h + 1) * 128]

    def relay(kind, k, h):
        src, buf, ring, cores, ring_out, core_out, last = kind
        here, there = slot(k), slot(k + 1)
        a = 2 * core + h
        for side in (0, 1) if k else (1,):
            block = buf.at[a, here, side]
            wait(block, ring.at[here, side, h])
            send(block, block, core_out.at[here], cores.at[here, h], sibling)
            if k < last and k != 4:
                to = z_up if side else z_down
                send(block, buf.at[a, there, side], ring_out.at[k], ring.at[there, side, h], to)

    def pass_on(kind, k):
        src, buf, ring, cores, ring_out, core_out, last = kind
        here, there = slot(k), slot(k + 1)
        for h in range(2):
            for side in range(2):
                a = 2 * core + h
                to = z_up if side else z_down
                send(buf.at[a, here, side], buf.at[a, there, side], ring_out.at[k], ring.at[there, side, h], to)

    def have(kind, k, h):
        wait(kind[1].at[0, slot(k)], kind[3].at[slot(k), h])

    def partials(kind, s, j, h):
        src, buf = kind[0], kind[1]

        @pl.loop(0, 2)
        def _(p):
            a = 2 * lax.rem(core + p, 2) + h

            @pl.when(p == 1)
            def _():
                have(kind, s, h)

            rows = buf[a, s].reshape(256, src.shape[1])
            x = lax.dot_general(src[...], rows, (((1,), (1,)), ((), ())), preferred_element_type=F32)
            for b in range(2):
                f = (a // 2) * 4 + lax.rem(a, 2) + 2 * b
                tile = x[b * 128 : (b + 1) * 128]

                @pl.when(f == feat)
                def _():
                    own[j] = tile

                @pl.when(f != feat)
                def _():
                    stage[j, f] = tile.astype(BF16)
                    send(stage.at[j, f], rs.at[j, feat], rs_out.at[j], rs_in.at[j], (tok, f))

    def add_up(j):
        wait(rs.at[j, 0:7], rs_in.at[j])

        @pl.loop(0, 4)
        def _(i):
            rows = pl.ds(pl.multiple_of(i * 32, 32), 32)
            v = own[j, rows]
            for p in range(1, 8):
                v = v + rs[j, feat_peer(p), rows].astype(F32)
            total[j, rows] = v

    def norms(s):
        k, l = total[s], total[5 + s]
        weight = 2.0 if s in (1, 2, 3) else 1.0
        for i, v in enumerate((k * l, k * k, l * l)):
            v = weight * jnp.sum(v, axis=0, keepdims=True)
            red[0, i : i + 1] += v[:, :128] + v[:, 128:]

    def step_sums(s):
        add_up(5 + s)
        add_up(s)
        norms(s)

    launch(S, 0)
    launch(T, 1)
    red[0] = jnp.zeros((8, 128), F32)
    for s in range(5):
        for kind, j in ((S, 5 + s), (T, s)):
            late = kind is T and s == 4
            for h in range(2):
                relay(kind, s, h)
                if late and h == 1:
                    pass_on(S, 4)
                if late:
                    partials(kind, s, j, h)
            for h in () if late else range(2):
                partials(kind, s, j, h)
            if kind is S and s:
                step_sums(s - 1)
    step_sums(4)

    def tok_at(p, q):
        return tok_of(lax.rem(xl + p, 2), z, core), feat_peer(q)

    groups = (
        [tok_at(p, q) for p in range(2) for q in range(8) if p or q],
        [(tok_of(xl, z + p, lax.rem(core + q, 2)), feat) for q in range(2) for p in range(8) if p or q],
    )
    for g, peers in enumerate(groups):
        for i, device in enumerate(peers):
            send(red.at[g], redr.at[g, i], red_out.at[g], red_in.at[g], device)
        wait(redr.at[g], red_in.at[g])
        v = red[g]
        for i in range(15):
            v = v + redr[g, i]
        red[g + 1] = v

    cross, ksq, lsq = (jnp.sum(red[2, i : i + 1], axis=1, keepdims=True) for i in range(3))
    knorm = jnp.sqrt(ksq)
    lnorm = jnp.sqrt(lsq)
    loss_ref[...] = -cross / (knorm * lnorm)
    by_kern = -1.0 / (knorm * lnorm)
    by_lern = cross / (knorm * lnorm * lnorm * lnorm)

    def weights(s):
        return by_kern * total[s] + by_lern * total[5 + s]

    def tile_of(f):
        return ((f // 4) * 2 + lax.rem(f, 2)) * 2 + lax.rem(f, 4) // 2

    here = tile_of(feat)
    for s in (1, 2, 3):
        w = weights(s)
        wn[here, :, s * 256 : (s + 1) * 256] = w.astype(BF16)
        for side in range(2):
            i = 2 * (s - 1) + side
            tst[i] = jnp.transpose(w[:, side * 128 : (side + 1) * 128]).astype(BF16)
            to = (tok_of(1 - xl, z - s, xh), swapped) if side else (tok_of(xl, z + s, xh), swapped)
            send(tst.at[i], wt.at[swapped, :, i * 128 : (i + 1) * 128], tr_out.at[0], tr_in.at[0], to)
    for s in (0, 4):
        wn[here, :, s * 256 : (s + 1) * 256] = weights(s).astype(BF16)

    up = xh * 4 + lax.rem(y + 1, 4)
    down = xh * 4 + lax.rem(y + 3, 4)
    far = xh * 4 + lax.rem(y + 2, 4)

    def across(f):
        return lax.rem(f + 4, 8)

    N = (wn, tile_of, agn_out, agn_in)
    R = (wt, lambda f: f, agt_out, agt_in)

    def give(group, f, part, to, i):
        buf, place, out, into = group
        ref = buf.at[place(f)]
        if part is not None:
            ref = ref.at[part[0] : part[1]]
        send(ref, ref, out.at[0], into.at[i], (tok, to))

    def got(group, f, part, i):
        buf, place, out, into = group
        ref = buf.at[place(f)]
        if part is not None:
            ref = ref.at[part[0] : part[1]]
        wait(ref, into.at[i])

    def first(group):
        give(group, feat, None, across(feat), 2)
        give(group, feat, None, up, 0)
        give(group, feat, None, down, 1)

    def second(group):
        got(group, down, None, 0)
        give(group, down, HALVES[0], up, 3)
        give(group, down, REST, across(feat), 9)
        got(group, up, None, 1)
        give(group, up, HALVES[1], down, 4)
        give(group, up, REST, across(feat), 10)
        got(group, across(feat), None, 2)
        give(group, across(feat), MOST, up, 5)
        give(group, across(feat), MOST, down, 6)

    def third(group):
        for i, part in enumerate(HALVES):
            got(group, far, part, 3 + i)
            give(group, far, part, across(feat), 7 + i)

    def fourth(group):
        got(group, across(down), MOST, 5)
        got(group, across(down), REST, 9)
        got(group, across(up), MOST, 6)
        got(group, across(up), REST, 10)
        for i, part in enumerate(HALVES):
            got(group, across(far), part, 7 + i)

    def product(buf, plane, lo, hi):
        @pl.loop(0, 2)
        def _(p):
            a = 2 * plane + p
            depth = (hi - lo) * 256
            w = buf[pl.ds(2 * a, 2)].reshape(256, depth)
            grad_ref[...] += jnp.dot(w, sb[a, lo:hi].reshape(depth, DS // 8), preferred_element_type=F32)

    first(N)
    wait(wt.at[feat], tr_in.at[0])
    first(R)
    for h in range(2):
        relay(S, 5, h)
    second(N)
    second(R)
    for h in range(2):
        relay(S, 6, h)
    third(N)
    third(R)
    for h in range(2):
        relay(S, 7, h)
    grad_ref[...] = jnp.zeros_like(grad_ref)
    product(wn, xh, 0, 5)
    for k in (5, 6, 7):
        for h in range(2):
            have(S, k, h)
    product(wt, xh, 5, 8)
    fourth(N)
    product(wn, 1 - xh, 0, 5)
    fourth(R)
    product(wt, 1 - xh, 5, 8)

    for kind, index in ((S, 0), (T, 1)):
        src, buf, ring, cores, ring_out, core_out, last = kind
        wait(src, x_out.at[index])
        for k in range(last):
            wait(buf.at[0:2, 0], ring_out.at[k])
        for k in range(last + 1):
            wait(buf.at[0:2, 0], core_out.at[k])
    for j in range(10):
        wait(rs.at[j, 0:7], rs_out.at[j])
    for g, peers in enumerate(groups):
        wait(redr.at[g], red_out.at[g])
    wait(wt.at[0], tr_out.at[0])
    wait(wn.at[0:7], agn_out.at[0])
    wait(wt.at[0:7], agt_out.at[0])


def local(teacher, student):
    rows, dt = teacher.shape
    ds = student.shape[1]
    dma = pltpu.SemaphoreType.DMA
    loss, grad = pl.pallas_call(
        kernel,
        out_shape=(jax.ShapeDtypeStruct((1, 1), F32), jax.ShapeDtypeStruct((rows, ds), F32)),
        in_specs=[pl.BlockSpec(memory_space=pl.ANY)] * 2,
        out_specs=[pl.BlockSpec(memory_space=pltpu.VMEM)] * 2,
        scratch_shapes=[
            pltpu.VMEM((rows, dt), BF16),
            pltpu.VMEM((rows, ds), BF16),
            pltpu.VMEM((4, 5, 2, 128, dt), BF16),
            pltpu.VMEM((4, 8, 2, 128, ds), BF16),
            pltpu.VMEM((10, 8, 128, 256), BF16),
            pltpu.VMEM((10, 8, 128, 256), BF16),
            pltpu.VMEM((10, 128, 256), F32),
            pltpu.VMEM((10, 128, 256), F32),
            pltpu.VMEM((8, 128, 1280), BF16),
            pltpu.VMEM((8, 128, 768), BF16),
            pltpu.VMEM((6, 128, 128), BF16),
            pltpu.VMEM((3, 8, 128), F32),
            pltpu.VMEM((2, 15, 8, 128), F32),
            dma((5, 2, 2)), dma((5, 2)), dma((4,)), dma((5,)),
            dma((8, 2, 2)), dma((8, 2)), dma((7,)), dma((8,)), dma((2,)),
            dma((10,)), dma((10,)), dma((2,)), dma((2,)), dma((1,)), dma((1,)),
            dma((11,)), dma((1,)), dma((11,)), dma((1,)), dma((2,)),
        ],
        compiler_params=pltpu.CompilerParams(
            collective_id=0, has_side_effects=True, vmem_limit_bytes=60 * 2**20
        ),
        cost_estimate=pl.CostEstimate(flops=7 * 10**9, bytes_accessed=2 * 10**6, transcendentals=0),
    )(teacher, student)
    return loss.reshape(()), (2.0 * TOKENS * DS) * grad


def solution(mesh):
    placed = (P("tok", "feat"), P("tok", "feat"))
    return jax.shard_map(
        local, mesh=mesh, in_specs=placed, out_specs=(P(), P("tok", "feat")), check_vma=False
    )
```
